32 devices in a mesh: groups: 2 (over x), blk: 16 (over z, y, core).
Axes of the slice: x: 2, y: 2, z: 4, core: 2. Of those that a mesh axis runs over, the one named last changes fastest.
Arguments:
- fitted_slab: float32 [2048, 14400], P('blk', 'groups'), parts along dimension 1, may hold values from -0.8 to 0.8
- pair_list: int32 [16, 8], replicated, may hold values from -1 to 7, as said below
Outputs:
- exchange_band: float32 [4096, 1920], P(('groups', 'blk')), parts along dimension 0
The draws below stay inside these ranges and needn't reach their ends.
There are 2 independent parts, one for each index of `groups`. The reference program is written for one: setup_inputs(seed, part) draws one part's arguments, and reference() takes and returns one part's arrays. A program takes and returns all parts, laid end to end along the dimension named above; an argument that names none is the same for every part. Nothing has to cross between parts.
Inputs may be any that keep to these rules, and one draw needn't show every extreme that they name: `pair_list`: each row lists distinct offsets in increasing order, then -1 padding; offset 0 is always listed; a + d < 16 for every listed offset d of row a; row 0 lists all offsets.
All inputs are finite; a program needn't handle non-finite values.
Results may differ from the reference program's by a relative error of at most 0.0003.
Values sent between devices are 32-bit elements; how exact they have to be, the bound alone decides.
No kernel may reach another device: no remote copies, remote signals or barrier semaphores. Data moves between devices by JAX's collectives and lax.ppermute only.
A program may use at most 128 MiB of HBM per device.

```python
import jax
import jax.numpy as jnp
from jax import lax

BS = 128
NOCC = 1200
NAUX = 6
REACH = 7
NBLOCKS = 16
NBASIS = 2048


def draw_pair_list(key, part):
    key = jax.random.fold_in(key, 11)
    level_key, roll_key = jax.random.split(key)
    slot_count = REACH + 1
    density = jax.random.randint(level_key, (NBLOCKS, 1), 1, 9)
    rolled = jax.random.randint(roll_key, (NBLOCKS, slot_count), 0, 8)
    offset_grid = jnp.arange(slot_count, dtype=jnp.int32)[None, :]
    block_grid = jnp.arange(NBLOCKS, dtype=jnp.int32)[:, None]
    keep = (rolled < density) | (offset_grid == 0) | (block_grid == 0)
    keep = keep & (block_grid + offset_grid < NBLOCKS)
    score = jnp.where(keep, offset_grid, slot_count + offset_grid)
    ordered = jnp.argsort(score, axis=1, stable=True).astype(jnp.int32)
    kept_count = jnp.sum(keep.astype(jnp.int32), axis=1, keepdims=True)
    return jnp.where(offset_grid < kept_count, ordered, -1).astype(jnp.int32)


def block_levels(own_key, extent, cuts, smallest, top_value):
    gain, own = 1.0, jax.random.fold_in(own_key, 6)
    for position, blocks in cuts:
        draws = jnp.exp(jax.random.uniform(jax.random.fold_in(own, position), (blocks,), jnp.float32, smallest / len(cuts), top_value / len(cuts)))
        gain = gain * jnp.repeat(draws, extent[position] // blocks).reshape([-1 if axis == position else 1 for axis in range(len(extent))])
    return gain


def normal_values(own_key, shape, deviation, reach, shards=(), kind=jnp.bfloat16):
    result = deviation * jax.random.normal(own_key, shape, jnp.float32)
    if shards:
        result = result * block_levels(own_key, shape, shards, -0.22, 0.18)
    return jnp.clip(result, -reach, reach).astype(kind)


def setup_inputs(seed: int = 0, part: int = 0) -> dict:
    key_list = jax.random.split(jax.random.key(seed), 3)
    own_keys = jax.random.split(jax.random.fold_in(key_list[2], part), 3)
    return {
        "fitted_slab": normal_values(own_keys[0], (NBASIS, NAUX * NOCC), 0.1, 0.8, ((0, 16),), jnp.float32),
        "pair_list": draw_pair_list(jax.random.fold_in(key_list[2], 71), part),
    }


def reference(fitted_slab, pair_list):
    basis_count, width = fitted_slab.shape
    block_count = basis_count // BS
    max_offset = pair_list.shape[1] - 1
    fitted = fitted_slab.reshape(block_count, BS, width)
    offset_range = jnp.arange(max_offset + 1, dtype=jnp.int32)
    present = jnp.any(pair_list[:, :, None] == offset_range[None, None, :], axis=1).astype(jnp.float32)

    def one_block(index):
        targets = jnp.minimum(index + offset_range, block_count - 1).astype(jnp.int32)
        neighbours = jnp.take(fitted, targets, axis=0)
        own_rows = lax.dynamic_index_in_dim(fitted, index, 0, keepdims=False)
        products = jnp.einsum('mk,jnk->jmn', own_rows, neighbours, precision=lax.Precision.HIGHEST)
        return products * present[index][:, None, None]

    upper_band = lax.map(one_block, jnp.arange(block_count, dtype=jnp.int32))
    lower_slots = []
    for slot in range(max_offset):
        distance = max_offset - slot
        moved = jnp.concatenate([jnp.zeros((distance, BS, BS), jnp.float32), upper_band[:block_count - distance, distance]], 0)
        lower_slots.append(jnp.swapaxes(moved, 1, 2))
    band = jnp.concatenate([jnp.stack(lower_slots, 1), upper_band], 1)
    return band.transpose(0, 2, 1, 3).reshape(block_count * BS, (2 * max_offset + 1) * BS)
```

```python
import functools

import jax
import jax.numpy as jnp
from jax import lax
from jax.sharding import PartitionSpec as P

PLANE = 4


def body(count, fitted_slab, pair_list):
    rows, width = fitted_slab.shape
    reach = pair_list.shape[1] - 1
    slots = 2 * reach + 1
    me = lax.axis_index("blk")
    k = me % PLANE
    upper = k >= 2
    outer = (k == 0) | (k == 3)
    devices = range(count)

    def xor(block, t):
        return lax.ppermute(block, "blk", [(i, i ^ t) for i in devices])

    def some(block, t, sources):
        return lax.ppermute(block, "blk", [(i, i ^ t) for i in devices if i % PLANE in sources])

    def shift(block, step):
        return lax.ppermute(block, "blk", [(i, i + step) for i in devices if 0 <= i + step < count])

    up = functools.partial(shift, step=PLANE)
    down = functools.partial(shift, step=-PLANE)

    quarters = fitted_slab.T.reshape(PLANE, width // PLANE, rows)

    def quarter(index):
        return lax.dynamic_index_in_dim(quarters, index, 0, keepdims=False)

    own = quarter(k)
    cx = xor(quarter(k ^ 1), 1)
    q2, q3 = quarter(k ^ 2), quarter(k ^ 3)
    far_outer = some(q3, 3, (0, 3)) + some(q2, 2, (0, 3))
    far_inner = some(q3, 3, (1, 2)) + some(q2, 2, (1, 2))
    near_inner = jnp.where(outer, cx, own)
    near_outer = jnp.where(outer, own, cx)
    b0 = jnp.where(upper, far_outer, near_outer)
    b3 = jnp.where(upper, near_outer, far_outer)
    b1 = jnp.where(upper, far_inner, near_inner)
    b2 = jnp.where(upper, near_inner, far_inner)
    x2 = jnp.where(outer, far_inner, far_outer)
    x3 = jnp.where(outer, far_outer, far_inner)

    low_near, high_near = up(near_inner), down(near_inner)
    low3, high0 = up(b3), down(b0)
    low_far, high_far = up(far_inner), down(far_inner)
    low0, high3 = up(b0), down(b3)

    def dot(a, b):
        return lax.dot_general(a, b, (((0,), (0,)), ((), ())), precision=lax.Precision.HIGH)

    mine = jnp.concatenate([own, x2, cx, x3], 1)

    def core_sum(part):
        return part[: 2 * rows] + xor(part[2 * rows :], 1)

    first = core_sum(dot(mine, jnp.concatenate([b0, b1, b2, b3, low3, high0, low_near, high_near], 1)))
    first_in = xor(first[rows:], 2)
    done = first[:rows, : 6 * rows] + first_in[:, : 6 * rows]

    low1 = jnp.where(upper, low_far, low_near)
    low2 = jnp.where(upper, low_near, low_far)
    high1 = jnp.where(upper, high_far, high_near)
    high2 = jnp.where(upper, high_near, high_far)
    lows, highs = [low1, low2, low3], [high0, high1, high2]
    cross = dot(jnp.concatenate(lows, 1), jnp.concatenate(highs, 1))

    def at(i, j):
        return cross[(i - 1) * rows : i * rows, j * rows : (j + 1) * rows]

    packs = jnp.stack(
        [
            jnp.concatenate([at(i, m) if m < i else at(m + 1, i).T for m in range(PLANE - 1)], 1)
            for i in range(PLANE)
        ]
    )
    packs = jnp.concatenate([lax.dynamic_index_in_dim(packs, k ^ t, 0, keepdims=False) for t in (0, 2, 1, 3)], 0)
    second = core_sum(jnp.concatenate([packs, dot(mine, jnp.concatenate([low_far, high_far], 1))], 1))
    second_in = xor(second[rows:], 2)
    pack = second[:rows, : 3 * rows] + second_in[:, : 3 * rows]
    from_high, from_low = down(pack), up(pack)

    third = core_sum(dot(mine, jnp.concatenate([low0, high3], 1)))
    third = third[:rows] + xor(third[rows:], 2)

    def col(array, i):
        return array[:, i * rows : (i + 1) * rows]

    low_n = col(first[:rows], 6) + col(second_in, 3)
    high_n = col(first[:rows], 7) + col(second_in, 4)
    low_f = col(first_in, 6) + col(second[:rows], 3)
    high_f = col(first_in, 7) + col(second[:rows], 4)
    wide = [
        col(from_low, 0),
        col(from_low, 0),
        col(from_low, 1),
        col(from_low, 2),
        col(third, 0),
        jnp.where(upper, low_f, low_n),
        jnp.where(upper, low_n, low_f),
        col(done, 4),
        col(done, 0),
        col(done, 1),
        col(done, 2),
        col(done, 3),
        col(done, 5),
        jnp.where(upper, high_f, high_n),
        jnp.where(upper, high_n, high_f),
        col(third, 1),
        col(from_high, 0),
        col(from_high, 1),
        col(from_high, 2),
    ]
    band = lax.dynamic_slice_in_dim(jnp.concatenate(wide, 1), (k + 1) * rows, slots * rows, 1)

    offsets = jnp.arange(reach + 1, dtype=jnp.int32)
    present = jnp.any(pair_list[:, :, None] == offsets, axis=1)
    padded = jnp.pad(present, ((reach, 0), (0, 0)))
    window = lax.dynamic_slice_in_dim(padded, me, reach + 1, 0)
    lower = [window[reach - d, d] for d in range(reach, 0, -1)]
    mask = jnp.concatenate([jnp.stack(lower), window[reach]])
    return jnp.where(jnp.repeat(mask, rows)[None, :], band, 0.0)


def solution(mesh):
    return jax.shard_map(
        functools.partial(body, mesh.shape["blk"]),
        mesh=mesh,
        in_specs=(P("blk", "groups"), P()),
        out_specs=P(("groups", "blk"), None),
        check_vma=False,
    )
```

```python
import functools

import jax
import jax.numpy as jnp
from jax import lax
from jax.experimental import pallas as pl
from jax.experimental.pallas import tpu as pltpu
from jax.sharding import PartitionSpec as P

PLANE = 4
VMEM_BYTES = 44 * 2**20


def halves(value):
    high = value.astype(jnp.bfloat16)
    return high, (value - high.astype(jnp.float32)).astype(jnp.bfloat16)


def product(a, b):
    dot = functools.partial(
        lax.dot_general,
        dimension_numbers=(((0,), (0,)), ((), ())),
        preferred_element_type=jnp.float32,
    )
    (ah, al), (bh, bl) = halves(a), halves(b)
    return dot(ah, bh) + (dot(ah, bl) + dot(al, bh))


def side_by_side(*values):
    return jnp.concatenate(values, 1)


def block(index, size):
    if isinstance(index, int):
        return slice(index * size, (index + 1) * size)
    return pl.ds(pl.multiple_of(index * size, size), size)


def spread(value, keep, other, send):
    rows = keep.shape[0]
    keep[...] = value[:rows]
    other[...] = value[rows : 2 * rows]
    send[...] = value[2 * rows :]


def sides(odd, even_pair, odd_pair):
    first, second = even_pair[...], odd_pair[...]
    return jnp.where(odd, first, second), jnp.where(odd, second, first)


def first_kernel(at_ref, own, x2, cx, x3, e0, o0, keep, other, send):
    k, odd = at_ref[0], at_ref[1] == 1
    rows = own.shape[1]
    mine = side_by_side(own[...], x2[...], cx[...], x3[...])
    out = product(mine, side_by_side(mine, *sides(odd, e0, o0)))
    for ref, r in ((keep, 0), (other, rows), (send, 2 * rows)):
        size = ref.shape[0]
        for i, t in enumerate((0, 2, 1, 3)):
            ref[:, block(k ^ t, rows)] = out[r : r + size, block(i, rows)]
        ref[:, PLANE * rows :] = out[r : r + size, PLANE * rows :]


def cross_kernel(at_ref, e0, o0, e1, o1, e2, o2, keep, other, send, packs):
    k, odd = at_ref[0], at_ref[1] == 1
    rows = e0.shape[1]
    upper = k >= 2
    low, high = zip(sides(odd, e0, o0), sides(odd, e1, o1), sides(odd, e2, o2))
    swap = k == 1
    low_1 = jnp.where(upper, low[2], low[0])
    low_2 = jnp.where(upper, low[0], jnp.where(swap, low[1], low[2]))
    low_3 = jnp.where(swap, low[2], low[1])
    swap = k == 2
    high_0 = jnp.where(swap, high[2], high[1])
    high_1 = jnp.where(upper, jnp.where(swap, high[1], high[2]), high[0])
    high_2 = jnp.where(upper, high[0], high[2])
    cross = product(side_by_side(low_1, low_2, low_3), side_by_side(high_0, high_1, high_2))

    def at(i, j):
        return cross[block(i - 1, rows), block(j, rows)]

    for i in range(PLANE):
        t = i ^ k
        place = jnp.where(t == 1, 2, jnp.where(t == 2, 1, t))
        for m in range(PLANE - 1):
            value = at(i, m) if m < i else at(m + 1, i).T
            packs[block(place, rows), block(m, rows)] = value
    spread(packs[...], keep, other, send)


def second_kernel(at_ref, own, x2, cx, x3, e1, o1, e2, o2, keep, other, send):
    k, odd = at_ref[0], at_ref[1] == 1
    (low_1, high_1), (low_2, high_2) = sides(odd, e1, o1), sides(odd, e2, o2)
    columns = (
        jnp.where(k == 1, low_2, low_1),
        jnp.where(k == 1, low_1, low_2),
        jnp.where(k == 2, high_2, high_1),
        jnp.where(k == 2, high_1, high_2),
    )
    mine = side_by_side(own[...], x2[...], cx[...], x3[...])
    spread(product(mine, side_by_side(*columns)), keep, other, send)


def third_kernel(at_ref, own, x2, cx, x3, e3, o3, keep, other, send):
    odd = at_ref[1] == 1
    rows = own.shape[1]
    mine = side_by_side(own[...], x2[...], cx[...], x3[...])
    out = product(side_by_side(*sides(odd, e3, o3)), mine)
    keep[...] = out[:, :rows]
    other[...] = out[:, rows : 2 * rows]
    send[...] = out[:, 2 * rows :]


def final_kernel(reach, at_ref, pairs, k1, c1, y1, k2, c2, y2, k3, c3, y3, ez, oz, out):
    k, odd, me = at_ref[0], at_ref[1] == 1, at_ref[2]
    rows = out.shape[0]
    upper = k >= 2
    from_low, from_high = sides(odd, ez, oz)

    def near(keep, core, i):
        return keep[:, block(i, rows)] + core[:rows, block(i, rows)]

    def whole(keep, core, far, i):
        return near(keep, core, i) + far[:, block(i, rows)]

    def write(index, value):
        slot = index - k - 1
        offset = slot - reach
        row = me + jnp.minimum(offset, 0)
        wanted = jnp.abs(offset)
        found = pairs[jnp.maximum(row, 0), 0] == wanted
        for m in range(1, reach + 1):
            found = found | (pairs[jnp.maximum(row, 0), m] == wanted)
        factor = jnp.where(found & (row >= 0), 1.0, 0.0)

        @pl.when((slot >= 0) & (slot <= 2 * reach))
        def _():
            out[:, block(slot, rows)] = value * factor

    for m in range(PLANE - 1):
        write(m + 1, from_low[:, block(m, rows)])
        write(4 * PLANE + m, from_high[:, block(m, rows)])
    for i in range(PLANE):
        write(2 * PLANE + i, whole(k1, c1, y1, i))
    inner = jnp.where(upper, 1, 0)
    for plane, i, j in ((1, 4, 1), (3, 5, 3)):
        write(plane * PLANE + 1 + inner, near(k1, c1, i) + y2[:, block(j, rows)])
        write(plane * PLANE + 2 - inner, near(k2, c2, j) + y1[:, block(i, rows)])
    write(2 * PLANE - 1, whole(k2, c2, y2, 0))
    write(3 * PLANE, whole(k2, c2, y2, 2))
    third = k3[...] + c3[:, :rows] + y3[...]
    write(PLANE, third[:rows].T)
    write(4 * PLANE - 1, third[rows:].T)


def call(kernel, outs, scratch, scalars, arrays):
    return pl.pallas_call(
        kernel,
        cost_estimate=pl.CostEstimate(flops=1000, bytes_accessed=1000, transcendentals=0),
        in_specs=[pl.BlockSpec(memory_space=pltpu.SMEM)] * len(scalars)
        + [pl.BlockSpec(memory_space=pltpu.VMEM)] * len(arrays),
        out_specs=[pl.BlockSpec(memory_space=pltpu.VMEM)] * len(outs),
        out_shape=outs,
        scratch_shapes=scratch,
        compiler_params=pltpu.CompilerParams(vmem_limit_bytes=VMEM_BYTES),
    )(*scalars, *arrays)


def after(value, *others):
    return lax.optimization_barrier((value, *others))[0]


def body(count, fitted_slab, pair_list):
    rows, width = fitted_slab.shape
    depth = width // PLANE
    reach = pair_list.shape[1] - 1
    me = lax.axis_index("blk").astype(jnp.int32)
    k = me % PLANE
    odd = (me // PLANE) % 2
    place = jnp.stack([k, odd, me])
    upper = k >= 2
    outer = (k == 0) | (k == 3)
    flip = upper ^ (odd == 1)
    devices = range(count)

    def xor(value, t):
        return lax.ppermute(value, "blk", [(i, i ^ t) for i in devices])

    def along(value, parity):
        route = []
        for i in devices:
            j = i + (PLANE if i // PLANE % 2 == parity else -PLANE)
            if j in devices:
                route.append((i, j))
        return lax.ppermute(value, "blk", route)

    def both(to_even, to_odd):
        return along(to_even, 0), along(to_odd, 1)

    quarters = fitted_slab.T.reshape(PLANE, depth, rows)

    def quarter(index, *others):
        return lax.dynamic_index_in_dim(after(quarters, *others), index, 0, keepdims=False)

    q1 = quarter(k ^ 1)
    cx = xor(q1, 1)
    q3 = quarter(k ^ 3, q1)
    x3 = xor(q3, 3)
    own = quarter(k, q1)
    near_inner = jnp.where(outer, cx, own)
    e0, o0 = both(near_inner, near_inner)
    x2 = xor(quarter(k ^ 2, cx), 2)

    own_a, cx_a, x3_a, _ = lax.optimization_barrier((own, cx, x3, near_inner))
    near_outer = jnp.where(outer, own_a, cx_a)
    e1, o1 = both(jnp.where(flip, near_outer, x3_a), jnp.where(flip, x3_a, near_outer))

    own_b, cx_b, x3_b, x2_b, _, _ = lax.optimization_barrier((own_a, cx_a, x3_a, x2, e0, o0))
    far_inner = jnp.where(outer, x2_b, x3_b)
    e2, o2 = both(jnp.where(flip, far_inner, x2_b), jnp.where(flip, x2_b, far_inner))

    own_c, cx_c, x3_c, x2_c, _, _ = lax.optimization_barrier((own_b, cx_b, x3_b, x2_b, e1, o1))
    near_outer = jnp.where(outer, own_c, cx_c)
    far_outer = jnp.where(outer, x3_c, x2_c)
    e3, o3 = both(jnp.where(flip, far_outer, near_outer), jnp.where(flip, near_outer, far_outer))

    def f32(*shape):
        return jax.ShapeDtypeStruct(shape, jnp.float32)

    def parts(n):
        return [f32(rows, n * rows), f32(rows, n * rows), f32(2 * rows, n * rows)]

    def core_sum(other, send):
        core = xor(send, 1)
        return core, other + core[rows:]

    def fenced(function, *operands):
        shapes = jax.eval_shape(function, *operands)

        def never(*_):
            return jax.tree.map(lambda x: jnp.zeros(x.shape, x.dtype), shapes)

        return lax.cond(me >= 0, function, never, *operands)

    mine = (own, x2, cx, x3)

    def first_part(place, *operands):
        keep, other, send = call(first_kernel, parts(6), [], (place,), operands)
        return (keep, *core_sum(other, send))

    k1, c1, out1 = fenced(first_part, place, *mine, e0, o0)
    y1 = xor(out1, 2)

    def second_part(place, own, x2, cx, x3, *arrived):
        keep, other, send = call(
            cross_kernel, parts(3), [pltpu.VMEM((PLANE * rows, 3 * rows), jnp.float32)], (place,), arrived
        )
        core, out = core_sum(other, send)
        pack = keep + core[:rows] + xor(out, 2)
        place = after(place, keep)
        keep, other, send = call(second_kernel, parts(4), [], (place,), (own, x2, cx, x3, *arrived[2:]))
        return pack, keep, *core_sum(other, send)

    pack, k2, c2, out2 = fenced(second_part, place, *mine, e0, o0, e1, o1, e2, o2)
    ez, oz = both(pack, pack)
    y2 = xor(out2, 2)

    e3, o3, _, _ = lax.optimization_barrier((e3, o3, pack, y1))
    pair = f32(2 * rows, rows)
    k3, other, send = call(third_kernel, [pair, pair, f32(2 * rows, 2 * rows)], [], (place,), (*mine, e3, o3))
    c3 = xor(send, 1)
    y3 = xor(after(other + c3[:, rows:], y2), 2)

    return call(
        functools.partial(final_kernel, reach),
        [f32(rows, (2 * reach + 1) * rows)],
        [],
        (place, pair_list),
        (k1, c1, y1, k2, c2, y2, k3, c3, y3, ez, oz),
    )[0]


def solution(mesh):
    return jax.shard_map(
        functools.partial(body, mesh.shape["blk"]),
        mesh=mesh,
        in_specs=(P("blk", "groups"), P()),
        out_specs=P(("groups", "blk"), None),
        check_vma=False,
    )
```

```python
import functools

import jax
import jax.numpy as jnp
from jax import lax
from jax.experimental import pallas as pl
from jax.experimental.pallas import tpu as pltpu
from jax.sharding import PartitionSpec as P

PLANE = 4
VMEM_BYTES = 44 * 2**20


def halves(value):
    high = value.astype(jnp.bfloat16)
    return high, (value - high.astype(jnp.float32)).astype(jnp.bfloat16)


def product(a, b):
    dot = functools.partial(
        lax.dot_general,
        dimension_numbers=(((0,), (0,)), ((), ())),
        preferred_element_type=jnp.float32,
    )
    (ah, al), (bh, bl) = halves(a), halves(b)
    return dot(ah, bh) + (dot(ah, bl) + dot(al, bh))


def side_by_side(*values):
    return jnp.concatenate(values, 1)


def block(index, size):
    if isinstance(index, int):
        return slice(index * size, (index + 1) * size)
    return pl.ds(pl.multiple_of(index * size, size), size)


def spread(value, keep, other, send):
    rows = keep.shape[0]
    keep[...] = value[:rows]
    other[...] = value[rows : 2 * rows]
    send[...] = value[2 * rows :]


def place_columns(value, keep, other, send, places):
    rows = keep.shape[0]
    for ref, r in ((keep, 0), (other, rows), (send, 2 * rows)):
        for i, index in enumerate(places):
            ref[:, block(index, rows)] = value[r : r + ref.shape[0], block(i, rows)]


def clear_column(keep, other, send, index):
    rows = keep.shape[0]
    for ref in (keep, other, send):
        ref[:, block(index, rows)] = jnp.zeros((ref.shape[0], rows), ref.dtype)


def first_kernel(at_ref, own, x2, cx, x3, e0, o0, e1, o1, keep, other, send):
    k, flip = at_ref[0], at_ref[2] == 1
    mine = side_by_side(own[...], x2[...], cx[...], x3[...])
    out = product(mine, side_by_side(mine, e0[...], o0[...], e1[...], o1[...]))
    first = jnp.where((k == 1) | (k == 2), 8, 7)
    even = jnp.where(flip, first, 6)
    place_columns(out, keep, other, send, (k, k ^ 2, k ^ 1, k ^ 3, 4, 5, even, 6 + first - even))
    clear_column(keep, other, send, 15 - first)


def add_kernel(a, b, out):
    out[...] = a[...] + b[...]


def cross_kernel(at_ref, e0, o0, e1, o1, e2, o2, keep, other, send, cross, packs):
    k, odd = at_ref[0], at_ref[1] == 1
    rows = e0.shape[1]
    cross[...] = product(side_by_side(e0[...], e1[...], e2[...]), side_by_side(o0[...], o1[...], o2[...]))
    upper = k >= 2
    low_2 = jnp.where(upper, 0, jnp.where(k == 1, 1, 2))
    low = (None, jnp.where(upper, 2, 0), low_2, jnp.where(k == 1, 2, 1))
    high_1 = jnp.where(upper, jnp.where(k == 2, 1, 2), 0)
    high = (jnp.where(k == 2, 2, 1), high_1, jnp.where(upper, 0, 2))

    def put(owner, m, value):
        t = owner ^ k
        place = jnp.where(t == 1, 2, jnp.where(t == 2, 1, t))
        packs[block(place, rows), block(m, rows)] = value

    for i in range(1, PLANE):
        for j in range(i):
            r, c = jnp.where(odd, low[i], high[j]), jnp.where(odd, high[j], low[i])
            value = cross[block(r, rows), block(c, rows)]
            turned = value.T
            put(i, j, jnp.where(odd, value, turned))
            put(j, i - 1, jnp.where(odd, turned, value))
    spread(packs[...], keep, other, send)


def second_kernel(at_ref, own, x2, cx, x3, e2, o2, keep, other, send):
    k, flip = at_ref[0], at_ref[2] == 1
    mine = side_by_side(own[...], x2[...], cx[...], x3[...])
    out = product(mine, side_by_side(e2[...], o2[...]))
    last = jnp.where((k == 1) | (k == 2), 0, 1)
    even = jnp.where(flip, last, 2)
    place_columns(out, keep, other, send, (even, 2 + last - even))
    clear_column(keep, other, send, 1 - last)


def third_kernel(own, x2, cx, x3, e3, o3, keep, other, send):
    rows = own.shape[1]
    mine = side_by_side(own[...], x2[...], cx[...], x3[...])
    out = product(side_by_side(e3[...], o3[...]), mine)
    keep[...] = out[:, :rows]
    other[...] = out[:, rows : 2 * rows]
    send[...] = out[:, 2 * rows :]


def wanted(pairs, me, offset, reach):
    row = me + jnp.minimum(offset, 0)
    distance = jnp.abs(offset)
    found = pairs[jnp.maximum(row, 0), 0] == distance
    for m in range(1, reach + 1):
        found = found | (pairs[jnp.maximum(row, 0), m] == distance)
    return jnp.where(found & (row >= 0), 1.0, 0.0)


def band_kernel(reach, at_ref, pairs, t1, y1, t2, y2, out):
    k, flip, me = at_ref[0], at_ref[2], at_ref[3]
    rows = out.shape[0]
    upper = k >= 2

    def write(index, *terms):
        slot = index - k - 1
        total = functools.reduce(jnp.add, [ref[:, block(i, rows)] for ref, i in terms])
        out[:, block(slot, rows)] = total * wanted(pairs, me, slot - reach, reach)

    for i in range(PLANE):
        write(2 * PLANE + i, (t1, i), (y1, i))
    low, high = PLANE, 3 * PLANE
    here, there = jnp.where(upper, high, low), jnp.where(upper, low, high)
    near = jnp.where(upper, 2, 1)
    this, that = 5 - flip, 4 + flip
    write(here + near, (t1, this), (y2, 2))
    write(there + near, (t1, that), (y2, 1), (y1, 8))
    write(here + 3 - near, (t2, 1), (t1, 8), (y1, this))
    write(there + 3 - near, (t2, 2), (y1, that))
    write(jnp.where(upper, high, low + 3), (t2, 0), (t1, 7), (y1, 6))
    write(jnp.where(upper, low + 3, high), (t1, 6), (y1, 7), (y2, 0))


def final_kernel(reach, at_ref, pairs, k3, c3, y3, ez, oz, band, out, parts, sems):
    del band
    k, odd, me = at_ref[0], at_ref[1] == 1, at_ref[3]
    rows = y3.shape[1]
    copies = []

    def write(index, value):
        slot, i = index - k - 1, len(copies)
        parts[i] = value * wanted(pairs, me, slot - reach, reach)
        copies.append(pltpu.make_async_copy(parts.at[i], out.at[:, block(slot, rows)], sems.at[i]))
        copies[-1].start()

    for m in range(PLANE - 1):
        behind = m >= k
        value = jnp.where(behind == odd, ez[:, block(m, rows)], oz[:, block(m, rows)])
        write(jnp.where(behind, m + 1, 4 * PLANE + m), value)
    third = k3[...] + c3[:, :rows] + y3[...]
    write(jnp.where(odd, PLANE, 4 * PLANE - 1), third[:rows].T)
    write(jnp.where(odd, 4 * PLANE - 1, PLANE), third[rows:].T)
    for copy in copies:
        copy.wait()


def call(kernel, outs, scratch, scalars, arrays, flops=1000):
    return pl.pallas_call(
        kernel,
        cost_estimate=pl.CostEstimate(flops=flops, bytes_accessed=1000, transcendentals=0),
        in_specs=[pl.BlockSpec(memory_space=pltpu.SMEM)] * len(scalars)
        + [pl.BlockSpec(memory_space=pltpu.VMEM)] * len(arrays),
        out_specs=[pl.BlockSpec(memory_space=pltpu.VMEM)] * len(outs),
        out_shape=outs,
        scratch_shapes=scratch,
        compiler_params=pltpu.CompilerParams(vmem_limit_bytes=VMEM_BYTES),
    )(*scalars, *arrays)


def after(value, *others):
    return lax.optimization_barrier((value, *others))[0]


def body(count, fitted_slab, pair_list):
    rows, width = fitted_slab.shape
    depth = width // PLANE
    reach = pair_list.shape[1] - 1
    me = lax.axis_index("blk").astype(jnp.int32)
    k = me % PLANE
    odd = (me // PLANE) % 2
    upper = k >= 2
    outer = (k == 0) | (k == 3)
    flip = upper ^ (odd == 1)
    place = jnp.stack([k, odd, flip.astype(jnp.int32), me])
    devices = range(count)

    def xor(value, t):
        return lax.ppermute(value, "blk", [(i, i ^ t) for i in devices])

    def along(value, parity):
        route = []
        for i in devices:
            j = i + (PLANE if i // PLANE % 2 == parity else -PLANE)
            if j in devices:
                route.append((i, j))
        return lax.ppermute(value, "blk", route)

    def both(to_even, to_odd):
        return along(to_even, 0), along(to_odd, 1)

    quarters = fitted_slab.T.reshape(PLANE, depth, rows)

    def quarter(index, *others):
        return lax.dynamic_index_in_dim(after(quarters, *others), index, 0, keepdims=False)

    q1 = quarter(k ^ 1)
    cx = xor(q1, 1)
    q3 = quarter(k ^ 3, q1)
    x3 = xor(q3, 3)
    own = quarter(k, q1)
    near_inner = jnp.where(outer, cx, own)
    e0, o0 = both(near_inner, near_inner)
    x2 = xor(quarter(k ^ 2, cx), 2)

    own_a, cx_a, x3_a, _ = lax.optimization_barrier((own, cx, x3, near_inner))
    near_outer = jnp.where(outer, own_a, cx_a)
    e1, o1 = both(jnp.where(flip, near_outer, x3_a), jnp.where(flip, x3_a, near_outer))

    own_b, cx_b, x3_b, x2_b, _, _ = lax.optimization_barrier((own_a, cx_a, x3_a, x2, e0, o0))
    far_inner = jnp.where(outer, x2_b, x3_b)
    e2, o2 = both(jnp.where(flip, far_inner, x2_b), jnp.where(flip, x2_b, far_inner))

    own_c, cx_c, x3_c, x2_c, _, _ = lax.optimization_barrier((own_b, cx_b, x3_b, x2_b, e1, o1))
    near_outer = jnp.where(outer, own_c, cx_c)
    far_outer = jnp.where(outer, x3_c, x2_c)
    e3, o3 = both(jnp.where(flip, far_outer, near_outer), jnp.where(flip, near_outer, far_outer))

    def f32(*shape):
        return jax.ShapeDtypeStruct(shape, jnp.float32)

    def parts(n):
        return [f32(rows, n * rows), f32(rows, n * rows), f32(2 * rows, n * rows)]

    def core_sum(keep, other, send):
        core = xor(send, 1)
        return keep + core[:rows], other + core[rows:]

    def fenced(function, *operands):
        shapes = jax.eval_shape(function, *operands)

        def never(*_):
            return jax.tree.map(lambda x: jnp.zeros(x.shape, x.dtype), shapes)

        return lax.cond(me >= 0, function, never, *operands)

    mine = (own, x2, cx, x3)

    def first_part(place, *operands):
        return core_sum(*call(first_kernel, parts(9), [], (place,), operands))

    t1, out1 = fenced(first_part, place, *mine, e0, o0, e1, o1)
    y1 = xor(out1, 2)

    def second_part(place, own, x2, cx, x3, *arrived):
        square, tall = (pltpu.VMEM((n * rows, 3 * rows), jnp.float32) for n in (PLANE - 1, PLANE))
        keep, other, send = call(cross_kernel, parts(3), [square, tall], (place,), arrived)
        half, out = core_sum(keep, other, send)
        far = xor(out, 2)
        pack = call(add_kernel, [f32(rows, 3 * rows)], [], (), (half, far), flops=10**11)[0]
        place = after(place, keep)
        return pack, *core_sum(*call(second_kernel, parts(3), [], (place,), (own, x2, cx, x3, *arrived[4:])))

    pack, t2, out2 = fenced(second_part, place, *mine, e0, o0, e1, o1, e2, o2)
    ez, oz = both(pack, pack)
    y2 = xor(out2, 2)

    e3, o3, _, _ = lax.optimization_barrier((e3, o3, pack, y1))
    pair = f32(2 * rows, rows)
    k3, other, send = call(third_kernel, [pair, pair, f32(2 * rows, 2 * rows)], [], (), (*mine, e3, o3))
    c3 = xor(after(send, y2), 1)
    y3 = xor(other + c3[:, rows:], 2)

    whole = f32(rows, (2 * reach + 1) * rows)
    band = call(functools.partial(band_kernel, reach), [whole], [], (place, pair_list), (t1, y1, t2, y2))[0]
    late = (k3, c3, y3, ez, oz)
    return pl.pallas_call(
        functools.partial(final_kernel, reach),
        in_specs=[pl.BlockSpec(memory_space=pltpu.SMEM)] * 2
        + [pl.BlockSpec(memory_space=pltpu.VMEM)] * len(late)
        + [pl.BlockSpec(memory_space=pl.ANY)],
        out_specs=pl.BlockSpec(memory_space=pl.ANY),
        out_shape=whole,
        scratch_shapes=[pltpu.VMEM((PLANE + 1, rows, rows), jnp.float32), pltpu.SemaphoreType.DMA((PLANE + 1,))],
        input_output_aliases={2 + len(late): 0},
        compiler_params=pltpu.CompilerParams(vmem_limit_bytes=VMEM_BYTES),
    )(place, pair_list, *late, band)


def solution(mesh):
    return jax.shard_map(
        functools.partial(body, mesh.shape["blk"]),
        mesh=mesh,
        in_specs=(P("blk", "groups"), P()),
        out_specs=P(("groups", "blk"), None),
        check_vma=False,
    )
```

```python
import functools

import jax
import jax.numpy as jnp
from jax import lax
from jax.experimental import pallas as pl
from jax.experimental.pallas import tpu as pltpu
from jax.sharding import PartitionSpec as P

PLANE = 4
VMEM_BYTES = 22 * 2**20


def halves(value):
    high = value.astype(jnp.bfloat16)
    return high, (value - high.astype(jnp.float32)).astype(jnp.bfloat16)


def product(a, b):
    dot = functools.partial(
        lax.dot_general,
        dimension_numbers=(((0,), (0,)), ((), ())),
        preferred_element_type=jnp.float32,
    )
    (ah, al), (bh, bl) = halves(a), halves(b)
    return dot(ah, bh) + (dot(ah, bl) + dot(al, bh))


def side_by_side(*values):
    return jnp.concatenate(values, 1)


def block(index, size):
    if isinstance(index, int):
        return slice(index * size, (index + 1) * size)
    return pl.ds(pl.multiple_of(index * size, size), size)


def spread(value, keep, other, send):
    rows = keep.shape[0]
    keep[...] = value[:rows]
    other[...] = value[rows : 2 * rows]
    send[...] = value[2 * rows :]


def place_columns(value, keep, other, send, places):
    rows = keep.shape[0]
    for ref, r in ((keep, 0), (other, rows), (send, 2 * rows)):
        for i, index in enumerate(places):
            ref[:, block(index, rows)] = value[r : r + ref.shape[0], block(i, rows)]


def clear_column(keep, other, send, index):
    rows = keep.shape[0]
    for ref in (keep, other, send):
        ref[:, block(index, rows)] = jnp.zeros((ref.shape[0], rows), ref.dtype)


def first_kernel(at_ref, own, x2, cx, x3, e0, o0, e1, o1, keep, other, send):
    k, flip = at_ref[0], at_ref[2] == 1
    mine = side_by_side(own[...], x2[...], cx[...], x3[...])
    out = product(mine, side_by_side(mine, e0[...], o0[...], e1[...], o1[...]))
    first = jnp.where((k == 1) | (k == 2), 8, 7)
    even = jnp.where(flip, first, 6)
    place_columns(out, keep, other, send, (k, k ^ 2, k ^ 1, k ^ 3, 4, 5, even, 6 + first - even))
    clear_column(keep, other, send, 15 - first)


def copy_kernel(a, out):
    out[...] = a[...]


def add_kernel(a, b, out):
    out[...] = a[...] + b[...]


def cross_kernel(at_ref, e0, o0, e1, o1, e2, o2, keep, other, send, cross, packs):
    k, odd = at_ref[0], at_ref[1] == 1
    rows = e0.shape[1]
    cross[...] = product(side_by_side(e0[...], e1[...], e2[...]), side_by_side(o0[...], o1[...], o2[...]))
    upper = k >= 2
    low_2 = jnp.where(upper, 0, jnp.where(k == 1, 1, 2))
    low = (None, jnp.where(upper, 2, 0), low_2, jnp.where(k == 1, 2, 1))
    high_1 = jnp.where(upper, jnp.where(k == 2, 1, 2), 0)
    high = (jnp.where(k == 2, 2, 1), high_1, jnp.where(upper, 0, 2))

    def put(owner, m, value):
        t = owner ^ k
        place = jnp.where(t == 1, 2, jnp.where(t == 2, 1, t))
        packs[block(place, rows), block(m, rows)] = value

    for i in range(1, PLANE):
        for j in range(i):
            r, c = jnp.where(odd, low[i], high[j]), jnp.where(odd, high[j], low[i])
            value = cross[block(r, rows), block(c, rows)]
            turned = value.T
            put(i, j, jnp.where(odd, value, turned))
            put(j, i - 1, jnp.where(odd, turned, value))
    spread(packs[...], keep, other, send)


def second_kernel(at_ref, own, x2, cx, x3, e2, o2, early_keep, early_other, keep, other, send):
    k, flip = at_ref[0], at_ref[2] == 1
    mine = side_by_side(own[...], x2[...], cx[...], x3[...])
    out = product(mine, side_by_side(e2[...], o2[...]))
    last = jnp.where((k == 1) | (k == 2), 0, 1)
    even = jnp.where(flip, last, 2)
    place_columns(out, keep, other, send, (even, 2 + last - even))
    clear_column(keep, other, send, 1 - last)
    early = early_keep.shape[1]
    keep[:, :early] += early_keep[...]
    other[:, :early] += early_other[...]


def turn_kernel(own, x2, cx, x3, high, low):
    rows = own.shape[1]
    for i, ref in enumerate((own, x2, cx, x3)):
        high[block(i, rows)], low[block(i, rows)] = halves(ref[...].T)


def third_kernel(high, low, e3, o3, keep, other, send):
    ch, cl = halves(side_by_side(e3[...], o3[...]))
    dot = functools.partial(jnp.dot, preferred_element_type=jnp.float32)
    spread(dot(high[...], ch) + (dot(high[...], cl) + dot(low[...], ch)), keep, other, send)


def wanted(pairs, me, offset, reach):
    row = me + jnp.minimum(offset, 0)
    distance = jnp.abs(offset)
    found = pairs[jnp.maximum(row, 0), 0] == distance
    for m in range(1, reach + 1):
        found = found | (pairs[jnp.maximum(row, 0), m] == distance)
    return jnp.where(found & (row >= 0), 1.0, 0.0)


def band_kernel(reach, at_ref, pairs, t1, y1, t2, y2, out):
    k, flip, me = at_ref[0], at_ref[2], at_ref[3]
    rows = out.shape[0]
    upper = k >= 2

    def write(index, *terms):
        slot = index - k - 1
        total = functools.reduce(jnp.add, [ref[:, block(i, rows)] for ref, i in terms])
        out[:, block(slot, rows)] = total * wanted(pairs, me, slot - reach, reach)

    for i in range(PLANE):
        write(2 * PLANE + i, (t1, i), (y1, i))
    low, high = PLANE, 3 * PLANE
    here, there = jnp.where(upper, high, low), jnp.where(upper, low, high)
    near = jnp.where(upper, 2, 1)
    this, that = 5 - flip, 4 + flip
    write(here + near, (t1, this), (y2, 2))
    write(there + near, (t1, that), (y2, 1))
    write(here + 3 - near, (t2, 1), (y1, this))
    write(there + 3 - near, (t2, 2), (y1, that))
    write(jnp.where(upper, high, low + 3), (t2, 0), (y1, 6))
    write(jnp.where(upper, low + 3, high), (t1, 6), (y2, 0))


def final_kernel(reach, at_ref, pairs, k3, c3, y3, ez, oz, band, out, parts, sems):
    del band
    k, odd, me = at_ref[0], at_ref[1] == 1, at_ref[3]
    rows = y3.shape[0]
    copies = []

    def write(index, value):
        slot, i = index - k - 1, len(copies)
        parts[i] = value * wanted(pairs, me, slot - reach, reach)
        copies.append(pltpu.make_async_copy(parts.at[i], out.at[:, block(slot, rows)], sems.at[i]))
        copies[-1].start()

    for m in range(PLANE - 1):
        behind = m >= k
        value = jnp.where(behind == odd, ez[:, block(m, rows)], oz[:, block(m, rows)])
        write(jnp.where(behind, m + 1, 4 * PLANE + m), value)
    third = k3[...] + c3[:rows] + y3[...]
    write(jnp.where(odd, PLANE, 4 * PLANE - 1), third[:, :rows])
    write(jnp.where(odd, 4 * PLANE - 1, PLANE), third[:, rows:])
    for copy in copies:
        copy.wait()


def call(kernel, outs, scratch, scalars, arrays, flops=1000):
    return pl.pallas_call(
        kernel,
        cost_estimate=pl.CostEstimate(flops=flops, bytes_accessed=sum(a.size * 4 for a in arrays), transcendentals=0),
        in_specs=[pl.BlockSpec(memory_space=pltpu.SMEM)] * len(scalars)
        + [pl.BlockSpec(memory_space=pltpu.VMEM)] * len(arrays),
        out_specs=[pl.BlockSpec(memory_space=pltpu.VMEM)] * len(outs),
        out_shape=outs,
        scratch_shapes=scratch,
        compiler_params=pltpu.CompilerParams(vmem_limit_bytes=VMEM_BYTES),
    )(*scalars, *arrays)


def after(value, *others):
    return lax.optimization_barrier((value, *others))[0]


def body(count, fitted_slab, pair_list):
    rows, width = fitted_slab.shape
    depth = width // PLANE
    reach = pair_list.shape[1] - 1
    me = lax.axis_index("blk").astype(jnp.int32)
    k = me % PLANE
    odd = (me // PLANE) % 2
    upper = k >= 2
    outer = (k == 0) | (k == 3)
    flip = upper ^ (odd == 1)
    place = jnp.stack([k, odd, flip.astype(jnp.int32), me])
    devices = range(count)

    def xor(value, t):
        return lax.ppermute(value, "blk", [(i, i ^ t) for i in devices])

    def along(value, parity):
        route = []
        for i in devices:
            j = i + (PLANE if i // PLANE % 2 == parity else -PLANE)
            if j in devices:
                route.append((i, j))
        return lax.ppermute(value, "blk", route)

    def both(to_even, to_odd):
        return along(to_even, 0), along(to_odd, 1)

    quarters = fitted_slab.T.reshape(PLANE, depth, rows)

    def quarter(index, *others):
        return lax.dynamic_index_in_dim(after(quarters, *others), index, 0, keepdims=False)

    q1 = quarter(k ^ 1)
    cx = xor(q1, 1)
    q3 = quarter(k ^ 3, q1)
    x3 = xor(q3, 3)
    own = quarter(k, q1)
    near_inner = jnp.where(outer, cx, own)
    e0, o0 = both(near_inner, near_inner)
    q2 = quarter(k ^ 2, cx)
    x2 = xor(q2, 2)

    own_a, cx_a, x3_a, _, _ = lax.optimization_barrier((own, cx, x3, near_inner, q2))
    near_outer = jnp.where(outer, own_a, cx_a)
    e1, o1 = both(jnp.where(flip, near_outer, x3_a), jnp.where(flip, x3_a, near_outer))

    own_b, cx_b, x3_b, x2_b, _, _ = lax.optimization_barrier((own_a, cx_a, x3_a, x2, e0, o0))
    far_inner = jnp.where(outer, x2_b, x3_b)
    e2, o2 = both(jnp.where(flip, far_inner, x2_b), jnp.where(flip, x2_b, far_inner))

    own_c, cx_c, x3_c, x2_c, _, _ = lax.optimization_barrier((own_b, cx_b, x3_b, x2_b, e1, o1))
    near_outer = jnp.where(outer, own_c, cx_c)
    far_outer = jnp.where(outer, x3_c, x2_c)
    e3, o3 = both(jnp.where(flip, far_outer, near_outer), jnp.where(flip, near_outer, far_outer))

    def f32(*shape):
        return jax.ShapeDtypeStruct(shape, jnp.float32)

    def parts(n):
        return [f32(rows, n * rows), f32(rows, n * rows), f32(2 * rows, n * rows)]

    def core_sum(keep, other, send):
        core = xor(send, 1)
        return keep + core[:rows], other + core[rows:]

    def fenced(function, *operands):
        shapes = jax.eval_shape(function, *operands)

        def never(*_):
            return jax.tree.map(lambda x: jnp.zeros(x.shape, x.dtype), shapes)

        return lax.cond(me >= 0, function, never, *operands)

    mine = (own, x2, cx, x3)

    def first_part(place, *operands):
        total, out = core_sum(*call(first_kernel, parts(9), [], (place,), operands))
        cut = 7 * rows
        return total[:, :cut], out[:, :cut], total[:, cut:], out[:, cut:]

    t1, out1, *early = fenced(first_part, place, *mine, e0, o0, e1, o1)
    y1 = xor(out1, 2)

    def second_part(place, own, x2, cx, x3, early_keep, early_other, *arrived):
        square, tall = (pltpu.VMEM((n * rows, 3 * rows), jnp.float32) for n in (PLANE - 1, PLANE))
        keep, other, send = call(cross_kernel, parts(3), [square, tall], (place,), arrived)
        half, out = core_sum(keep, other, send)
        far = xor(out, 2)
        place = after(place, out)
        k2, other, send = call(second_kernel, parts(3), [], (place,), (own, x2, cx, x3, *arrived[4:], early_keep, early_other))
        turned = [jax.ShapeDtypeStruct((PLANE * rows, depth), jnp.bfloat16)] * 2
        high, low = call(turn_kernel, turned, [], (), (after(own, k2), x2, cx, x3))
        half = after(half, high)
        pack = call(add_kernel, [f32(rows, 3 * rows)], [], (), (half, far), flops=10**11)[0]
        return pack, high, low, *core_sum(k2, other, send)

    pack, high, low, t2, out2 = fenced(second_part, place, *mine, *early, e0, o0, e1, o1, e2, o2)
    ez, oz = both(pack, pack)
    y2 = xor(out2, 2)

    e3, o3, _, _ = lax.optimization_barrier((e3, o3, pack, y1))
    k3, other, send = call(third_kernel, parts(2), [], (), (high, low, e3, o3))
    c3 = xor(send, 1)
    y2 = call(copy_kernel, [f32(rows, 3 * rows)], [], (), (y2,), flops=5 * 10**9)[0]
    y3 = xor(after(other + c3[rows:], y2), 2)

    whole = f32(rows, (2 * reach + 1) * rows)
    band = call(functools.partial(band_kernel, reach), [whole], [], (place, pair_list), (t1, y1, t2, y2))[0]
    late = (k3, c3, y3, ez, oz)
    return pl.pallas_call(
        functools.partial(final_kernel, reach),
        in_specs=[pl.BlockSpec(memory_space=pltpu.SMEM)] * 2
        + [pl.BlockSpec(memory_space=pltpu.VMEM)] * len(late)
        + [pl.BlockSpec(memory_space=pl.ANY)],
        out_specs=pl.BlockSpec(memory_space=pl.ANY),
        out_shape=whole,
        scratch_shapes=[pltpu.VMEM((PLANE + 1, rows, rows), jnp.float32), pltpu.SemaphoreType.DMA((PLANE + 1,))],
        input_output_aliases={2 + len(late): 0},
        compiler_params=pltpu.CompilerParams(vmem_limit_bytes=VMEM_BYTES),
    )(place, pair_list, *late, band)


def solution(mesh):
    return jax.shard_map(
        functools.partial(body, mesh.shape["blk"]),
        mesh=mesh,
        in_specs=(P("blk", "groups"), P()),
        out_specs=P(("groups", "blk"), None),
        check_vma=False,
    )
```

```python
import functools

import jax
import jax.numpy as jnp
from jax import lax
from jax.experimental import pallas as pl
from jax.experimental.pallas import tpu as pltpu
from jax.sharding import PartitionSpec as P

PLANE = 4
VMEM_BYTES = 22 * 2**20


def halves(value):
    high = value.astype(jnp.bfloat16)
    return high, (value - high.astype(jnp.float32)).astype(jnp.bfloat16)


def product(a, b):
    dot = functools.partial(
        lax.dot_general,
        dimension_numbers=(((0,), (0,)), ((), ())),
        preferred_element_type=jnp.float32,
    )
    (ah, al), (bh, bl) = halves(a), halves(b)
    width = b.shape[1]
    main = dot(ah, side_by_side(bh, bl))
    return main[:, :width] + (main[:, width:] + dot(al, bh))


def side_by_side(*values):
    return jnp.concatenate(values, 1)


def block(index, size):
    if isinstance(index, int):
        return slice(index * size, (index + 1) * size)
    return pl.ds(pl.multiple_of(index * size, size), size)


def spread(value, keep, other, send):
    rows = keep.shape[0]
    keep[...] = value[:rows]
    other[...] = value[rows : 2 * rows]
    send[...] = value[2 * rows :]


def place_columns(value, keep, other, send, places):
    rows = keep.shape[0]
    for ref, r in ((keep, 0), (other, rows), (send, 2 * rows)):
        for i, index in enumerate(places):
            ref[:, block(index, rows)] = value[r : r + ref.shape[0], block(i, rows)]


def clear_column(keep, other, send, index):
    rows = keep.shape[0]
    for ref in (keep, other, send):
        ref[:, block(index, rows)] = jnp.zeros((ref.shape[0], rows), ref.dtype)


def early_kernel(own, cx, x3, e0, o0, out):
    mine = side_by_side(own[...], cx[...], x3[...])
    out[...] = product(mine, side_by_side(mine, e0[...], o0[...]))


def first_kernel(
    at_ref, known, own, x2, cx, x3, e0, o0, e1, o1, keep, other, early_keep, early_other, send
):
    k, flip = at_ref[0], at_ref[2] == 1
    rows = own.shape[1]
    fresh = product(
        side_by_side(own[...], x2[...], cx[...], x3[...]), side_by_side(x2[...], e1[...], o1[...])
    )
    beside = product(x2[...], side_by_side(e0[...], o0[...]))

    def new(i, j):
        return fresh[block(i, rows), block(j, rows)]

    def line(i, j):
        old = [known[block(j, rows), block(c, rows)] for c in range(5)]
        return side_by_side(old[0], new(i, 0), *old[1:], new(i, 1), new(i, 2))

    second = side_by_side(new(0, 0).T, new(1, 0), new(2, 0).T, new(3, 0).T, beside, new(1, 1), new(1, 2))
    out = jnp.concatenate([line(0, 0), second, line(2, 1), line(3, 2)], 0)
    first = jnp.where((k == 1) | (k == 2), 2, 1)
    even = jnp.where(flip, first, 0)
    near, far = (k, k ^ 2, k ^ 1, k ^ 3, 4, 5), (even, first - even)
    cut = len(near) * rows
    place_columns(out[:, :cut], keep, other, send, near)
    place_columns(out[:, cut:], early_keep, early_other, send.at[:, cut:], far)
    clear_column(early_keep, early_other, send.at[:, cut:], 3 - first)


def copy_kernel(a, out):
    out[...] = a[...]


def add_kernel(a, b, out):
    out[...] = a[...] + b[...]


def cross_kernel(at_ref, e0, o0, e1, o1, e2, o2, keep, other, send, cross, packs):
    k, odd = at_ref[0], at_ref[1] == 1
    rows = e0.shape[1]
    cross[...] = product(side_by_side(e0[...], e1[...], e2[...]), side_by_side(o0[...], o1[...], o2[...]))
    upper = k >= 2
    low_2 = jnp.where(upper, 0, jnp.where(k == 1, 1, 2))
    low = (None, jnp.where(upper, 2, 0), low_2, jnp.where(k == 1, 2, 1))
    high_1 = jnp.where(upper, jnp.where(k == 2, 1, 2), 0)
    high = (jnp.where(k == 2, 2, 1), high_1, jnp.where(upper, 0, 2))

    def put(owner, m, value):
        t = owner ^ k
        place = jnp.where(t == 1, 2, jnp.where(t == 2, 1, t))
        packs[block(place, rows), block(m, rows)] = value

    for i in range(1, PLANE):
        for j in range(i):
            r, c = jnp.where(odd, low[i], high[j]), jnp.where(odd, high[j], low[i])
            value = cross[block(r, rows), block(c, rows)]
            turned = value.T
            put(i, j, jnp.where(odd, value, turned))
            put(j, i - 1, jnp.where(odd, turned, value))
    spread(packs[...], keep, other, send)


def second_kernel(at_ref, own, x2, cx, x3, e2, o2, early_keep, early_other, keep, other, send):
    k, flip = at_ref[0], at_ref[2] == 1
    mine = side_by_side(own[...], x2[...], cx[...], x3[...])
    out = product(mine, side_by_side(e2[...], o2[...]))
    last = jnp.where((k == 1) | (k == 2), 1, 2)
    even = jnp.where(flip, last, 3)
    place_columns(out, keep, other, send, (even, 3 + last - even))
    clear_column(keep, other, send, 0)
    clear_column(keep, other, send, 3 - last)
    early = early_keep.shape[1]
    keep[:, :early] += early_keep[...]
    other[:, :early] += early_other[...]


def turn_kernel(own, x2, cx, x3, high, low):
    rows = own.shape[1]
    for i, ref in enumerate((own, x2, cx, x3)):
        high[block(i, rows)], low[block(i, rows)] = halves(ref[...].T)


def third_kernel(high, low, e3, o3, keep, other, send):
    ch, cl = halves(side_by_side(e3[...], o3[...]))
    dot = functools.partial(jnp.dot, preferred_element_type=jnp.float32)
    spread(dot(high[...], ch) + (dot(high[...], cl) + dot(low[...], ch)), keep, other, send)


def wanted(pairs, me, offset, reach):
    row = me + jnp.minimum(offset, 0)
    distance = jnp.abs(offset)
    found = pairs[jnp.maximum(row, 0), 0] == distance
    for m in range(1, reach + 1):
        found = found | (pairs[jnp.maximum(row, 0), m] == distance)
    return jnp.where(found & (row >= 0), 1.0, 0.0)


def band_kernel(reach, at_ref, pairs, t1, y1, t2, y2, out):
    k, flip, me = at_ref[0], at_ref[2], at_ref[3]
    rows = out.shape[0]
    upper = k >= 2

    def write(index, *terms):
        slot = index - k - 1
        total = functools.reduce(jnp.add, [ref[:, block(i, rows)] for ref, i in terms])
        out[:, block(slot, rows)] = total * wanted(pairs, me, slot - reach, reach)

    for i in range(PLANE):
        write(2 * PLANE + i, (t1, i), (y1, i))
    low, high = PLANE, 3 * PLANE
    here, there = jnp.where(upper, high, low), jnp.where(upper, low, high)
    near = jnp.where(upper, 2, 1)
    this, that = 5 - flip, 4 + flip
    write(here + near, (t1, this), (y2, 3))
    write(there + near, (t1, that), (y2, 2))
    write(here + 3 - near, (t2, 2), (y1, this))
    write(there + 3 - near, (t2, 3), (y1, that))
    write(jnp.where(upper, high, low + 3), (t2, 1), (y2, 0))
    write(jnp.where(upper, low + 3, high), (t2, 0), (y2, 1))


def final_kernel(reach, at_ref, pairs, k3, c3, y3, ez, oz, band, out, parts, sems):
    del band
    k, odd, me = at_ref[0], at_ref[1] == 1, at_ref[3]
    rows = y3.shape[0]
    copies = []

    def write(index, value):
        slot, i = index - k - 1, len(copies)
        parts[i] = value * wanted(pairs, me, slot - reach, reach)
        copies.append(pltpu.make_async_copy(parts.at[i], out.at[:, block(slot, rows)], sems.at[i]))
        copies[-1].start()

    for m in range(PLANE - 1):
        behind = m >= k
        value = jnp.where(behind == odd, ez[:, block(m, rows)], oz[:, block(m, rows)])
        write(jnp.where(behind, m + 1, 4 * PLANE + m), value)
    third = k3[...] + c3[:rows] + y3[...]
    write(jnp.where(odd, PLANE, 4 * PLANE - 1), third[:, :rows])
    write(jnp.where(odd, 4 * PLANE - 1, PLANE), third[:, rows:])
    for copy in copies:
        copy.wait()


def call(kernel, outs, scratch, scalars, arrays, flops=1000):
    return pl.pallas_call(
        kernel,
        cost_estimate=pl.CostEstimate(flops=flops, bytes_accessed=sum(a.size * 4 for a in arrays), transcendentals=0),
        in_specs=[pl.BlockSpec(memory_space=pltpu.SMEM)] * len(scalars)
        + [pl.BlockSpec(memory_space=pltpu.VMEM)] * len(arrays),
        out_specs=[pl.BlockSpec(memory_space=pltpu.VMEM)] * len(outs),
        out_shape=outs,
        scratch_shapes=scratch,
        compiler_params=pltpu.CompilerParams(vmem_limit_bytes=VMEM_BYTES),
    )(*scalars, *arrays)


def after(value, *others):
    return lax.optimization_barrier((value, *others))[0]


def body(count, fitted_slab, pair_list):
    rows, width = fitted_slab.shape
    depth = width // PLANE
    reach = pair_list.shape[1] - 1
    me = lax.axis_index("blk").astype(jnp.int32)
    k = me % PLANE
    odd = (me // PLANE) % 2
    upper = k >= 2
    outer = (k == 0) | (k == 3)
    flip = upper ^ (odd == 1)
    place = jnp.stack([k, odd, flip.astype(jnp.int32), me])
    devices = range(count)

    def xor(value, t):
        return lax.ppermute(value, "blk", [(i, i ^ t) for i in devices])

    def along(value, parity):
        route = []
        for i in devices:
            j = i + (PLANE if i // PLANE % 2 == parity else -PLANE)
            if j in devices:
                route.append((i, j))
        return lax.ppermute(value, "blk", route)

    def both(to_even, to_odd):
        second = along(to_odd, 1)
        return along(to_even, 0), second

    def f32(*shape):
        return jax.ShapeDtypeStruct(shape, jnp.float32)

    quarters = fitted_slab.T.reshape(PLANE, depth, rows)

    def quarter(index, *others):
        return lax.dynamic_index_in_dim(after(quarters, *others), index, 0, keepdims=False)

    q1 = quarter(k ^ 1)
    cx = xor(q1, 1)
    q3 = quarter(k ^ 3, q1)
    x3 = xor(q3, 3)
    own = quarter(k, q1)
    near_inner = jnp.where(outer, cx, own)
    e0, o0 = both(near_inner, near_inner)
    q2 = quarter(k ^ 2, cx)
    x2 = xor(q2, 2)

    own_a, cx_a, x3_a, _, _ = lax.optimization_barrier((own, cx, x3, near_inner, q2))
    near_outer = jnp.where(outer, own_a, cx_a)
    e1, o1 = both(jnp.where(flip, near_outer, x3_a), jnp.where(flip, x3_a, near_outer))

    known = call(early_kernel, [f32(3 * rows, 5 * rows)], [], (), (own, cx, x3, e0, o0))[0]
    own_b, cx_b, x3_b, x2_b, _ = lax.optimization_barrier((own_a, cx_a, x3_a, x2, known))
    far_inner = jnp.where(outer, x2_b, x3_b)
    e2, o2 = both(jnp.where(flip, far_inner, x2_b), jnp.where(flip, x2_b, far_inner))

    own_c, cx_c, x3_c, x2_c, _, _ = lax.optimization_barrier((own_b, cx_b, x3_b, x2_b, e1, o1))
    near_outer = jnp.where(outer, own_c, cx_c)
    far_outer = jnp.where(outer, x3_c, x2_c)
    e3, o3 = both(jnp.where(flip, far_outer, near_outer), jnp.where(flip, near_outer, far_outer))

    def parts(n):
        return [f32(rows, n * rows), f32(rows, n * rows), f32(2 * rows, n * rows)]

    def core_sum(keep, other, send):
        core = xor(send, 1)
        return keep + core[:rows], other + core[rows:]

    def fenced(function, *operands):
        shapes = jax.eval_shape(function, *operands)

        def never(*_):
            return jax.tree.map(lambda x: jnp.zeros(x.shape, x.dtype), shapes)

        return lax.cond(me >= 0, function, never, *operands)

    mine = (own, x2, cx, x3)

    def first_part(place, *operands):
        near, far, cut = parts(PLANE + 2), parts(3), (PLANE + 2) * rows
        outs = near[:2] + far[:2] + [f32(2 * rows, 9 * rows)]
        *kept, send = call(first_kernel, outs, [], (place,), operands)
        core = xor(send, 1)
        corner = core[:rows, :cut], core[rows:, :cut], core[:rows, cut:], core[rows:, cut:]
        return tuple(a + b for a, b in zip(kept, corner))

    t1, out1, *early = fenced(first_part, place, known, *mine, e0, o0, e1, o1)
    y1 = xor(out1, 2)

    def second_part(place, own, x2, cx, x3, early_keep, early_other, *arrived):
        square, tall = (pltpu.VMEM((n * rows, 3 * rows), jnp.float32) for n in (PLANE - 1, PLANE))
        keep, other, send = call(cross_kernel, parts(3), [square, tall], (place,), arrived)
        half, out = core_sum(keep, other, send)
        far = xor(out, 2)
        place = after(place, out)
        k2, other, send = call(second_kernel, parts(4), [], (place,), (own, x2, cx, x3, *arrived[4:], early_keep, early_other))
        turned = [jax.ShapeDtypeStruct((PLANE * rows, depth), jnp.bfloat16)] * 2
        high, low = call(turn_kernel, turned, [], (), (after(own, k2), x2, cx, x3))
        half = after(half, high)
        pack = call(add_kernel, [f32(rows, 3 * rows)], [], (), (half, far), flops=10**11)[0]
        return pack, high, low, *core_sum(k2, other, send)

    pack, high, low, t2, out2 = fenced(second_part, place, *mine, *early, e0, o0, e1, o1, e2, o2)
    ez, oz = both(pack, pack)
    y2 = xor(out2, 2)

    e3, o3, _, _ = lax.optimization_barrier((e3, o3, pack, y1))
    k3, other, send = call(third_kernel, parts(2), [], (), (high, low, e3, o3))
    c3 = xor(send, 1)
    y2 = call(copy_kernel, [f32(rows, 4 * rows)], [], (), (y2,), flops=5 * 10**9)[0]
    y3 = xor(after(other + c3[rows:], y2), 2)

    whole = f32(rows, (2 * reach + 1) * rows)
    band = call(functools.partial(band_kernel, reach), [whole], [], (place, pair_list), (t1, y1, t2, y2))[0]
    late = (k3, c3, y3, ez, oz)
    return pl.pallas_call(
        functools.partial(final_kernel, reach),
        in_specs=[pl.BlockSpec(memory_space=pltpu.SMEM)] * 2
        + [pl.BlockSpec(memory_space=pltpu.VMEM)] * len(late)
        + [pl.BlockSpec(memory_space=pl.ANY)],
        out_specs=pl.BlockSpec(memory_space=pl.ANY),
        out_shape=whole,
        scratch_shapes=[pltpu.VMEM((PLANE + 1, rows, rows), jnp.float32), pltpu.SemaphoreType.DMA((PLANE + 1,))],
        input_output_aliases={2 + len(late): 0},
        compiler_params=pltpu.CompilerParams(vmem_limit_bytes=VMEM_BYTES),
    )(place, pair_list, *late, band)


def solution(mesh):
    return jax.shard_map(
        functools.partial(body, mesh.shape["blk"]),
        mesh=mesh,
        in_specs=(P("blk", "groups"), P()),
        out_specs=P(("groups", "blk"), None),
        check_vma=False,
    )
```

```python
import functools

import jax
import jax.numpy as jnp
from jax import lax
from jax.experimental import pallas as pl
from jax.experimental.pallas import tpu as pltpu
from jax.sharding import PartitionSpec as P

PLANE = 4
VMEM_BYTES = 22 * 2**20


def halves(value):
    high = value.astype(jnp.bfloat16)
    return high, (value - high.astype(jnp.float32)).astype(jnp.bfloat16)


def product(a, b):
    dot = functools.partial(
        lax.dot_general,
        dimension_numbers=(((0,), (0,)), ((), ())),
        preferred_element_type=jnp.float32,
    )
    (ah, al), (bh, bl) = halves(a), halves(b)
    width = b.shape[1]
    main = dot(ah, side_by_side(bh, bl))
    return main[:, :width] + (main[:, width:] + dot(al, bh))


def side_by_side(*values):
    return jnp.concatenate(values, 1)


def block(index, size):
    if isinstance(index, int):
        return slice(index * size, (index + 1) * size)
    return pl.ds(pl.multiple_of(index * size, size), size)


def spread(value, keep, other, send):
    rows = keep.shape[0]
    keep[...] = value[:rows]
    other[...] = value[rows : 2 * rows]
    send[...] = value[2 * rows :]


def place_columns(value, keep, other, send, places):
    rows = keep.shape[0]
    for ref, r in ((keep, 0), (other, rows), (send, 2 * rows)):
        for i, index in enumerate(places):
            ref[:, block(index, rows)] = value[r : r + ref.shape[0], block(i, rows)]


def clear_column(keep, other, send, index):
    rows = keep.shape[0]
    for ref in (keep, other, send):
        ref[:, block(index, rows)] = jnp.zeros((ref.shape[0], rows), ref.dtype)


def early_kernel(own, cx, x3, e0, o0, out):
    mine = side_by_side(own[...], cx[...], x3[...])
    out[...] = product(mine, side_by_side(mine, e0[...], o0[...]))


def first_kernel(
    at_ref, known, own, x2, cx, x3, e0, o0, e1, o1, keep, other, early_keep, early_other, send
):
    k, flip = at_ref[0], at_ref[2] == 1
    rows = own.shape[1]
    fresh = product(
        side_by_side(own[...], x2[...], cx[...], x3[...]), side_by_side(x2[...], e1[...], o1[...])
    )
    beside = product(x2[...], side_by_side(e0[...], o0[...]))

    def new(i, j):
        return fresh[block(i, rows), block(j, rows)]

    def line(i, j):
        old = [known[block(j, rows), block(c, rows)] for c in range(5)]
        return side_by_side(old[0], new(i, 0), *old[1:], new(i, 1), new(i, 2))

    second = side_by_side(new(0, 0).T, new(1, 0), new(2, 0).T, new(3, 0).T, beside, new(1, 1), new(1, 2))
    out = jnp.concatenate([line(0, 0), second, line(2, 1), line(3, 2)], 0)
    first = jnp.where((k == 1) | (k == 2), 2, 1)
    even = jnp.where(flip, first, 0)
    near, far = (k, k ^ 2, k ^ 1, k ^ 3, 4, 5), (even, first - even)
    cut = len(near) * rows
    place_columns(out[:, :cut], keep, other, send, near)
    place_columns(out[:, cut:], early_keep, early_other, send.at[:, cut:], far)
    clear_column(early_keep, early_other, send.at[:, cut:], 3 - first)


def copy_kernel(a, out):
    out[...] = a[...]


def add_kernel(a, b, out):
    out[...] = a[...] + b[...]


def part_kernel(e0, o0, e1, o1, out):
    out[...] = product(side_by_side(e0[...], e1[...]), side_by_side(o0[...], o1[...]))


def cross_kernel(at_ref, known, e0, o0, e1, o1, e2, o2, keep, other, send, cross, packs):
    k, odd = at_ref[0], at_ref[1] == 1
    rows = e0.shape[1]
    two = known.shape[0]
    cross[:two, :two] = known[...]
    cross[two:] = product(e2[...], side_by_side(o0[...], o1[...], o2[...]))
    cross[:two, two:] = product(side_by_side(e0[...], e1[...]), o2[...])
    upper = k >= 2
    low_2 = jnp.where(upper, 0, jnp.where(k == 1, 1, 2))
    low = (None, jnp.where(upper, 2, 0), low_2, jnp.where(k == 1, 2, 1))
    high_1 = jnp.where(upper, jnp.where(k == 2, 1, 2), 0)
    high = (jnp.where(k == 2, 2, 1), high_1, jnp.where(upper, 0, 2))

    def put(owner, m, value):
        t = owner ^ k
        place = jnp.where(t == 1, 2, jnp.where(t == 2, 1, t))
        packs[block(place, rows), block(m, rows)] = value

    for i in range(1, PLANE):
        for j in range(i):
            r, c = jnp.where(odd, low[i], high[j]), jnp.where(odd, high[j], low[i])
            value = cross[block(r, rows), block(c, rows)]
            turned = value.T
            put(i, j, jnp.where(odd, value, turned))
            put(j, i - 1, jnp.where(odd, turned, value))
    spread(packs[...], keep, other, send)


def second_kernel(at_ref, own, x2, cx, x3, e2, o2, early_keep, early_other, keep, other, send):
    k, flip = at_ref[0], at_ref[2] == 1
    mine = side_by_side(own[...], x2[...], cx[...], x3[...])
    out = product(mine, side_by_side(e2[...], o2[...]))
    last = jnp.where((k == 1) | (k == 2), 1, 2)
    even = jnp.where(flip, last, 3)
    place_columns(out, keep, other, send, (even, 3 + last - even))
    clear_column(keep, other, send, 0)
    clear_column(keep, other, send, 3 - last)
    early = early_keep.shape[1]
    keep[:, :early] += early_keep[...]
    other[:, :early] += early_other[...]


def turn_kernel(own, x2, cx, x3, high, low):
    rows = own.shape[1]
    for i, ref in enumerate((own, x2, cx, x3)):
        high[block(i, rows)], low[block(i, rows)] = halves(ref[...].T)


def third_kernel(high, low, e3, o3, keep, other, send):
    ch, cl = halves(side_by_side(e3[...], o3[...]))
    dot = functools.partial(jnp.dot, preferred_element_type=jnp.float32)
    spread(dot(high[...], ch) + (dot(high[...], cl) + dot(low[...], ch)), keep, other, send)


def wanted(pairs, me, offset, reach):
    row = me + jnp.minimum(offset, 0)
    distance = jnp.abs(offset)
    found = pairs[jnp.maximum(row, 0), 0] == distance
    for m in range(1, reach + 1):
        found = found | (pairs[jnp.maximum(row, 0), m] == distance)
    return jnp.where(found & (row >= 0), 1.0, 0.0)


def band_kernel(reach, at_ref, pairs, t1, y1, t2, y2, out):
    k, flip, me = at_ref[0], at_ref[2], at_ref[3]
    rows = out.shape[0]
    upper = k >= 2

    def write(index, *terms):
        slot = index - k - 1
        total = functools.reduce(jnp.add, [ref[:, block(i, rows)] for ref, i in terms])
        out[:, block(slot, rows)] = total * wanted(pairs, me, slot - reach, reach)

    for i in range(PLANE):
        write(2 * PLANE + i, (t1, i), (y1, i))
    low, high = PLANE, 3 * PLANE
    here, there = jnp.where(upper, high, low), jnp.where(upper, low, high)
    near = jnp.where(upper, 2, 1)
    this, that = 5 - flip, 4 + flip
    write(here + near, (t1, this), (y2, 3))
    write(there + near, (t1, that), (y2, 2))
    write(here + 3 - near, (t2, 2), (y1, this))
    write(there + 3 - near, (t2, 3), (y1, that))
    write(jnp.where(upper, high, low + 3), (t2, 1), (y2, 0))
    write(jnp.where(upper, low + 3, high), (t2, 0), (y2, 1))


def final_kernel(reach, at_ref, pairs, k3, c3, y3, ez, oz, band, out, parts, sems):
    del band
    k, odd, me = at_ref[0], at_ref[1] == 1, at_ref[3]
    rows = y3.shape[0]
    copies = []

    def write(index, value):
        slot, i = index - k - 1, len(copies)
        parts[i] = value * wanted(pairs, me, slot - reach, reach)
        copies.append(pltpu.make_async_copy(parts.at[i], out.at[:, block(slot, rows)], sems.at[i]))
        copies[-1].start()

    for m in range(PLANE - 1):
        behind = m >= k
        value = jnp.where(behind == odd, ez[:, block(m, rows)], oz[:, block(m, rows)])
        write(jnp.where(behind, m + 1, 4 * PLANE + m), value)
    third = k3[...] + c3[:rows] + y3[...]
    write(jnp.where(odd, PLANE, 4 * PLANE - 1), third[:, :rows])
    write(jnp.where(odd, 4 * PLANE - 1, PLANE), third[:, rows:])
    for copy in copies:
        copy.wait()


def call(kernel, outs, scratch, scalars, arrays, flops=1000):
    return pl.pallas_call(
        kernel,
        cost_estimate=pl.CostEstimate(flops=flops, bytes_accessed=sum(a.size * 4 for a in arrays), transcendentals=0),
        in_specs=[pl.BlockSpec(memory_space=pltpu.SMEM)] * len(scalars)
        + [pl.BlockSpec(memory_space=pltpu.VMEM)] * len(arrays),
        out_specs=[pl.BlockSpec(memory_space=pltpu.VMEM)] * len(outs),
        out_shape=outs,
        scratch_shapes=scratch,
        compiler_params=pltpu.CompilerParams(vmem_limit_bytes=VMEM_BYTES),
    )(*scalars, *arrays)


def after(value, *others):
    return lax.optimization_barrier((value, *others))[0]


def body(count, fitted_slab, pair_list):
    rows, width = fitted_slab.shape
    depth = width // PLANE
    reach = pair_list.shape[1] - 1
    me = lax.axis_index("blk").astype(jnp.int32)
    k = me % PLANE
    odd = (me // PLANE) % 2
    upper = k >= 2
    outer = (k == 0) | (k == 3)
    flip = upper ^ (odd == 1)
    place = jnp.stack([k, odd, flip.astype(jnp.int32), me])
    devices = range(count)

    def xor(value, t):
        return lax.ppermute(value, "blk", [(i, i ^ t) for i in devices])

    def along(value, parity):
        route = []
        for i in devices:
            j = i + (PLANE if i // PLANE % 2 == parity else -PLANE)
            if j in devices:
                route.append((i, j))
        return lax.ppermute(value, "blk", route)

    def both(to_even, to_odd):
        second = along(to_odd, 1)
        return along(to_even, 0), second

    def f32(*shape):
        return jax.ShapeDtypeStruct(shape, jnp.float32)

    quarters = fitted_slab.T.reshape(PLANE, depth, rows)

    def quarter(index, *others):
        return lax.dynamic_index_in_dim(after(quarters, *others), index, 0, keepdims=False)

    q1 = quarter(k ^ 1)
    cx = xor(q1, 1)
    q3 = quarter(k ^ 3, q1)
    x3 = xor(q3, 3)
    own = quarter(k, q1)
    near_inner = jnp.where(outer, cx, own)
    e0, o0 = both(near_inner, near_inner)
    q2 = quarter(k ^ 2, cx)
    x2 = xor(q2, 2)

    own_a, cx_a, x3_a, _, _ = lax.optimization_barrier((own, cx, x3, near_inner, q2))
    near_outer = jnp.where(outer, own_a, cx_a)
    e1, o1 = both(jnp.where(flip, near_outer, x3_a), jnp.where(flip, x3_a, near_outer))

    known = call(early_kernel, [f32(3 * rows, 5 * rows)], [], (), (own, cx, x3, e0, o0))[0]
    own_b, cx_b, x3_b, x2_b, _ = lax.optimization_barrier((own_a, cx_a, x3_a, x2, known))
    far_inner = jnp.where(outer, x2_b, x3_b)
    e2, o2 = both(jnp.where(flip, far_inner, x2_b), jnp.where(flip, x2_b, far_inner))

    own_c, cx_c, x3_c, x2_c, _, _ = lax.optimization_barrier((own_b, cx_b, x3_b, x2_b, e1, o1))
    near_outer = jnp.where(outer, own_c, cx_c)
    far_outer = jnp.where(outer, x3_c, x2_c)
    e3, o3 = both(jnp.where(flip, far_outer, near_outer), jnp.where(flip, near_outer, far_outer))

    def parts(n):
        return [f32(rows, n * rows), f32(rows, n * rows), f32(2 * rows, n * rows)]

    def core_sum(keep, other, send):
        core = xor(send, 1)
        return keep + core[:rows], other + core[rows:]

    def fenced(function, *operands):
        shapes = jax.eval_shape(function, *operands)

        def never(*_):
            return jax.tree.map(lambda x: jnp.zeros(x.shape, x.dtype), shapes)

        return lax.cond(me >= 0, function, never, *operands)

    mine = (own, x2, cx, x3)

    def first_part(place, *operands):
        near, far, cut = parts(PLANE + 2), parts(3), (PLANE + 2) * rows
        outs = near[:2] + far[:2] + [f32(2 * rows, 9 * rows)]
        *kept, send = call(first_kernel, outs, [], (place,), operands)
        crossed = call(part_kernel, [f32(2 * rows, 2 * rows)], [], (), (after(operands[5], send), *operands[6:]))[0]
        core = xor(send, 1)
        corner = core[:rows, :cut], core[rows:, :cut], core[:rows, cut:], core[rows:, cut:]
        return crossed, *(a + b for a, b in zip(kept, corner))

    crossed, t1, out1, *early = fenced(first_part, place, known, *mine, e0, o0, e1, o1)
    y1 = xor(out1, 2)

    def second_part(place, crossed, own, x2, cx, x3, early_keep, early_other, *arrived):
        square, tall = (pltpu.VMEM((n * rows, 3 * rows), jnp.float32) for n in (PLANE - 1, PLANE))
        keep, other, send = call(cross_kernel, parts(3), [square, tall], (place,), (crossed, *arrived))
        half, out = core_sum(keep, other, send)
        far = xor(out, 2)
        place = after(place, out)
        k2, other, send = call(second_kernel, parts(4), [], (place,), (own, x2, cx, x3, *arrived[4:], early_keep, early_other))
        turned = [jax.ShapeDtypeStruct((PLANE * rows, depth), jnp.bfloat16)] * 2
        high, low = call(turn_kernel, turned, [], (), (after(own, k2), x2, cx, x3))
        half = after(half, high)
        pack = call(add_kernel, [f32(rows, 3 * rows)], [], (), (half, far), flops=10**11)[0]
        return pack, high, low, *core_sum(k2, other, send)

    pack, high, low, t2, out2 = fenced(second_part, place, crossed, *mine, *early, e0, o0, e1, o1, e2, o2)
    ez, oz = both(pack, pack)
    y2 = xor(out2, 2)

    e3, o3, _, _ = lax.optimization_barrier((e3, o3, pack, y1))
    k3, other, send = call(third_kernel, parts(2), [], (), (high, low, e3, o3))
    c3 = xor(send, 1)
    y2 = call(copy_kernel, [f32(rows, 4 * rows)], [], (), (y2,), flops=5 * 10**9)[0]
    y3 = xor(after(other + c3[rows:], y2), 2)

    whole = f32(rows, (2 * reach + 1) * rows)
    band = call(functools.partial(band_kernel, reach), [whole], [], (place, pair_list), (t1, y1, t2, y2))[0]
    late = (k3, c3, y3, ez, oz)
    return pl.pallas_call(
        functools.partial(final_kernel, reach),
        in_specs=[pl.BlockSpec(memory_space=pltpu.SMEM)] * 2
        + [pl.BlockSpec(memory_space=pltpu.VMEM)] * len(late)
        + [pl.BlockSpec(memory_space=pl.ANY)],
        out_specs=pl.BlockSpec(memory_space=pl.ANY),
        out_shape=whole,
        scratch_shapes=[pltpu.VMEM((PLANE + 1, rows, rows), jnp.float32), pltpu.SemaphoreType.DMA((PLANE + 1,))],
        input_output_aliases={2 + len(late): 0},
        compiler_params=pltpu.CompilerParams(vmem_limit_bytes=VMEM_BYTES),
    )(place, pair_list, *late, band)


def solution(mesh):
    return jax.shard_map(
        functools.partial(body, mesh.shape["blk"]),
        mesh=mesh,
        in_specs=(P("blk", "groups"), P()),
        out_specs=P(("groups", "blk"), None),
        check_vma=False,
    )
```

```python
import functools

import jax
import jax.numpy as jnp
from jax import lax
from jax.experimental import pallas as pl
from jax.experimental.pallas import tpu as pltpu
from jax.sharding import PartitionSpec as P

PLANE = 4
VMEM_BYTES = 22 * 2**20


def halves(value):
    high = value.astype(jnp.bfloat16)
    return high, (value - high.astype(jnp.float32)).astype(jnp.bfloat16)


def product(a, b):
    dot = functools.partial(
        lax.dot_general,
        dimension_numbers=(((0,), (0,)), ((), ())),
        preferred_element_type=jnp.float32,
    )
    (ah, al), (bh, bl) = halves(a), halves(b)
    width = b.shape[1]
    main = dot(ah, side_by_side(bh, bl))
    return main[:, :width] + (main[:, width:] + dot(al, bh))


def side_by_side(*values):
    return jnp.concatenate(values, 1)


def block(index, size):
    if isinstance(index, int):
        return slice(index * size, (index + 1) * size)
    return pl.ds(pl.multiple_of(index * size, size), size)


def spread(value, keep, other, send):
    rows = keep.shape[0]
    keep[...] = value[:rows]
    other[...] = value[rows : 2 * rows]
    send[...] = value[2 * rows :]


def place_columns(value, keep, other, send, places):
    rows = keep.shape[0]
    for ref, r in ((keep, 0), (other, rows), (send, 2 * rows)):
        for i, index in enumerate(places):
            ref[:, block(index, rows)] = value[r : r + ref.shape[0], block(i, rows)]


def clear_column(keep, other, send, index):
    rows = keep.shape[0]
    for ref in (keep, other, send):
        ref[:, block(index, rows)] = jnp.zeros((ref.shape[0], rows), ref.dtype)


def early_kernel(own, cx, x3, e0, o0, out):
    mine = side_by_side(own[...], cx[...], x3[...])
    out[...] = product(mine, side_by_side(mine, e0[...], o0[...]))


def first_kernel(
    at_ref, known, own, x2, cx, x3, e0, o0, e1, o1, keep, other, early_keep, early_other, send
):
    k, flip = at_ref[0], at_ref[2] == 1
    rows = own.shape[1]
    fresh = product(
        side_by_side(own[...], x2[...], cx[...], x3[...]), side_by_side(x2[...], e1[...], o1[...])
    )
    beside = product(x2[...], side_by_side(e0[...], o0[...]))

    def new(i, j):
        return fresh[block(i, rows), block(j, rows)]

    def line(i, j):
        old = [known[block(j, rows), block(c, rows)] for c in range(5)]
        return side_by_side(old[0], new(i, 0), *old[1:], new(i, 1), new(i, 2))

    second = side_by_side(new(0, 0).T, new(1, 0), new(2, 0).T, new(3, 0).T, beside, new(1, 1), new(1, 2))
    out = jnp.concatenate([line(0, 0), second, line(2, 1), line(3, 2)], 0)
    first = jnp.where((k == 1) | (k == 2), 2, 1)
    even = jnp.where(flip, first, 0)
    near, far = (k, k ^ 2, k ^ 1, k ^ 3, 4, 5), (even, first - even)
    cut = len(near) * rows
    place_columns(out[:, :cut], keep, other, send, near)
    place_columns(out[:, cut:], early_keep, early_other, send.at[:, cut:], far)
    clear_column(early_keep, early_other, send.at[:, cut:], 3 - first)


def copy_kernel(a, out):
    out[...] = a[...]


def add_kernel(a, b, out):
    out[...] = a[...] + b[...]


def turned_product(high, low, columns):
    ch, cl = halves(columns)
    dot = functools.partial(jnp.dot, preferred_element_type=jnp.float32)
    width = columns.shape[1]
    main = dot(high[...], side_by_side(ch, cl))
    return main[:, :width] + (main[:, width:] + dot(low[...], ch))


def part_kernel(e0, o0, e1, o1, out, high, low):
    rows = e0.shape[1]
    for i, ref in enumerate((e0, e1)):
        high[block(i, rows)], low[block(i, rows)] = halves(ref[...].T)
    out[...] = turned_product(high, low, side_by_side(o0[...], o1[...]))


def cross_kernel(at_ref, known, turned_high, turned_low, o0, o1, e2, o2, keep, other, send, cross, packs):
    k, odd = at_ref[0], at_ref[1] == 1
    rows = e2.shape[1]
    two = known.shape[0]
    cross[:two, :two] = known[...]
    cross[two:] = product(e2[...], side_by_side(o0[...], o1[...], o2[...]))
    cross[:two, two:] = turned_product(turned_high, turned_low, o2[...])
    upper = k >= 2
    low_2 = jnp.where(upper, 0, jnp.where(k == 1, 1, 2))
    low = (None, jnp.where(upper, 2, 0), low_2, jnp.where(k == 1, 2, 1))
    high_1 = jnp.where(upper, jnp.where(k == 2, 1, 2), 0)
    high = (jnp.where(k == 2, 2, 1), high_1, jnp.where(upper, 0, 2))

    def put(owner, m, value):
        t = owner ^ k
        place = jnp.where(t == 1, 2, jnp.where(t == 2, 1, t))
        packs[block(place, rows), block(m, rows)] = value

    for i in range(1, PLANE):
        for j in range(i):
            r, c = jnp.where(odd, low[i], high[j]), jnp.where(odd, high[j], low[i])
            value = cross[block(r, rows), block(c, rows)]
            turned = value.T
            put(i, j, jnp.where(odd, value, turned))
            put(j, i - 1, jnp.where(odd, turned, value))
    spread(packs[...], keep, other, send)


def second_kernel(at_ref, own, x2, cx, x3, e2, o2, early_keep, early_other, keep, other, send):
    k, flip = at_ref[0], at_ref[2] == 1
    mine = side_by_side(own[...], x2[...], cx[...], x3[...])
    out = product(mine, side_by_side(e2[...], o2[...]))
    last = jnp.where((k == 1) | (k == 2), 1, 2)
    even = jnp.where(flip, last, 3)
    place_columns(out, keep, other, send, (even, 3 + last - even))
    clear_column(keep, other, send, 0)
    clear_column(keep, other, send, 3 - last)
    early = early_keep.shape[1]
    keep[:, :early] += early_keep[...]
    other[:, :early] += early_other[...]


def turn_kernel(own, x2, cx, x3, high, low):
    rows = own.shape[1]
    for i, ref in enumerate((own, x2, cx, x3)):
        high[block(i, rows)], low[block(i, rows)] = halves(ref[...].T)


def third_kernel(high, low, e3, o3, keep, other, send):
    ch, cl = halves(side_by_side(e3[...], o3[...]))
    dot = functools.partial(jnp.dot, preferred_element_type=jnp.float32)
    spread(dot(high[...], ch) + (dot(high[...], cl) + dot(low[...], ch)), keep, other, send)


def wanted(pairs, me, offset, reach):
    row = me + jnp.minimum(offset, 0)
    distance = jnp.abs(offset)
    found = pairs[jnp.maximum(row, 0), 0] == distance
    for m in range(1, reach + 1):
        found = found | (pairs[jnp.maximum(row, 0), m] == distance)
    return jnp.where(found & (row >= 0), 1.0, 0.0)


def band_kernel(reach, at_ref, pairs, t1, y1, t2, y2, out):
    k, flip, me = at_ref[0], at_ref[2], at_ref[3]
    rows = out.shape[0]
    upper = k >= 2

    def write(index, *terms):
        slot = index - k - 1
        total = functools.reduce(jnp.add, [ref[:, block(i, rows)] for ref, i in terms])
        out[:, block(slot, rows)] = total * wanted(pairs, me, slot - reach, reach)

    for i in range(PLANE):
        write(2 * PLANE + i, (t1, i), (y1, i))
    low, high = PLANE, 3 * PLANE
    here, there = jnp.where(upper, high, low), jnp.where(upper, low, high)
    near = jnp.where(upper, 2, 1)
    this, that = 5 - flip, 4 + flip
    write(here + near, (t1, this), (y2, 3))
    write(there + near, (t1, that), (y2, 2))
    write(here + 3 - near, (t2, 2), (y1, this))
    write(there + 3 - near, (t2, 3), (y1, that))
    write(jnp.where(upper, high, low + 3), (t2, 1), (y2, 0))
    write(jnp.where(upper, low + 3, high), (t2, 0), (y2, 1))


def final_kernel(reach, at_ref, pairs, k3, c3, y3, ez, oz, band, out, parts, sems):
    del band
    k, odd, me = at_ref[0], at_ref[1] == 1, at_ref[3]
    rows = y3.shape[0]
    copies = []

    def write(index, value):
        slot, i = index - k - 1, len(copies)
        parts[i] = value * wanted(pairs, me, slot - reach, reach)
        copies.append(pltpu.make_async_copy(parts.at[i], out.at[:, block(slot, rows)], sems.at[i]))
        copies[-1].start()

    for m in range(PLANE - 1):
        behind = m >= k
        value = jnp.where(behind == odd, ez[:, block(m, rows)], oz[:, block(m, rows)])
        write(jnp.where(behind, m + 1, 4 * PLANE + m), value)
    third = k3[...] + c3[:rows] + y3[...]
    write(jnp.where(odd, PLANE, 4 * PLANE - 1), third[:, :rows])
    write(jnp.where(odd, 4 * PLANE - 1, PLANE), third[:, rows:])
    for copy in copies:
        copy.wait()


def call(kernel, outs, scratch, scalars, arrays, flops=1000):
    return pl.pallas_call(
        kernel,
        cost_estimate=pl.CostEstimate(flops=flops, bytes_accessed=sum(a.size * 4 for a in arrays), transcendentals=0),
        in_specs=[pl.BlockSpec(memory_space=pltpu.SMEM)] * len(scalars)
        + [pl.BlockSpec(memory_space=pltpu.VMEM)] * len(arrays),
        out_specs=[pl.BlockSpec(memory_space=pltpu.VMEM)] * len(outs),
        out_shape=outs,
        scratch_shapes=scratch,
        compiler_params=pltpu.CompilerParams(vmem_limit_bytes=VMEM_BYTES),
    )(*scalars, *arrays)


def after(value, *others):
    return lax.optimization_barrier((value, *others))[0]


def body(count, fitted_slab, pair_list):
    rows, width = fitted_slab.shape
    depth = width // PLANE
    reach = pair_list.shape[1] - 1
    me = lax.axis_index("blk").astype(jnp.int32)
    k = me % PLANE
    odd = (me // PLANE + 1) % 2
    upper = k >= 2
    outer = (k == 0) | (k == 3)
    flip = upper ^ (odd == 1)
    place = jnp.stack([k, odd, flip.astype(jnp.int32), me])
    devices = range(count)

    def xor(value, t):
        return lax.ppermute(value, "blk", [(i, i ^ t) for i in devices])

    def along(value, parity):
        route = []
        for i in devices:
            j = i + (PLANE if (i // PLANE + 1) % 2 == parity else -PLANE)
            if j in devices:
                route.append((i, j))
        return lax.ppermute(value, "blk", route)

    def both(to_even, to_odd):
        second = along(to_odd, 1)
        return along(to_even, 0), second

    def f32(*shape):
        return jax.ShapeDtypeStruct(shape, jnp.float32)

    quarters = fitted_slab.T.reshape(PLANE, depth, rows)

    def quarter(index, *others):
        return lax.dynamic_index_in_dim(after(quarters, *others), index, 0, keepdims=False)

    q1 = quarter(k ^ 1)
    cx = xor(q1, 1)
    q3 = quarter(k ^ 3, q1)
    x3 = xor(q3, 3)
    own = quarter(k, q1)
    near_inner = jnp.where(outer, cx, own)
    e0, o0 = both(near_inner, near_inner)
    q2 = quarter(k ^ 2, cx)
    x2 = xor(q2, 2)

    own_a, cx_a, x3_a, _, _ = lax.optimization_barrier((own, cx, x3, near_inner, q2))
    near_outer = jnp.where(outer, own_a, cx_a)
    e1, o1 = both(jnp.where(flip, near_outer, x3_a), jnp.where(flip, x3_a, near_outer))

    known = call(early_kernel, [f32(3 * rows, 5 * rows)], [], (), (own, cx, x3, e0, o0))[0]
    own_b, cx_b, x3_b, x2_b, _ = lax.optimization_barrier((own_a, cx_a, x3_a, x2, known))
    far_inner = jnp.where(outer, x2_b, x3_b)
    e2, o2 = both(jnp.where(flip, far_inner, x2_b), jnp.where(flip, x2_b, far_inner))

    own_c, cx_c, x3_c, x2_c, _, _ = lax.optimization_barrier((own_b, cx_b, x3_b, x2_b, e1, o1))
    near_outer = jnp.where(outer, own_c, cx_c)
    far_outer = jnp.where(outer, x3_c, x2_c)
    e3, o3 = both(jnp.where(flip, far_outer, near_outer), jnp.where(flip, near_outer, far_outer))

    def parts(n):
        return [f32(rows, n * rows), f32(rows, n * rows), f32(2 * rows, n * rows)]

    def core_sum(keep, other, send):
        core = xor(send, 1)
        return keep + core[:rows], other + core[rows:]

    def fenced(function, *operands):
        shapes = jax.eval_shape(function, *operands)

        def never(*_):
            return jax.tree.map(lambda x: jnp.zeros(x.shape, x.dtype), shapes)

        return lax.cond(me >= 0, function, never, *operands)

    mine = (own, x2, cx, x3)

    def first_part(place, *operands):
        near, far, cut = parts(PLANE + 2), parts(3), (PLANE + 2) * rows
        outs = near[:2] + far[:2] + [f32(2 * rows, 9 * rows)]
        *kept, send = call(first_kernel, outs, [], (place,), operands)
        turned = [jax.ShapeDtypeStruct((2 * rows, depth), jnp.bfloat16)] * 2
        arrived = (after(operands[5], send), *operands[6:])
        crossed = call(part_kernel, [f32(2 * rows, 2 * rows), *turned], [], (), arrived)
        core = xor(send, 1)
        corner = core[:rows, :cut], core[rows:, :cut], core[:rows, cut:], core[rows:, cut:]
        return *crossed, *(a + b for a, b in zip(kept, corner))

    *crossed, t1, out1, early_keep, early_other = fenced(first_part, place, known, *mine, e0, o0, e1, o1)
    y1 = xor(out1, 2)

    def second_part(place, crossed, own, x2, cx, x3, early_keep, early_other, *arrived):
        square, tall = (pltpu.VMEM((n * rows, 3 * rows), jnp.float32) for n in (PLANE - 1, PLANE))
        keep, other, send = call(cross_kernel, parts(3), [square, tall], (place,), (*crossed, *arrived))
        half, out = core_sum(keep, other, send)
        far = xor(out, 2)
        place = after(place, out)
        k2, other, send = call(second_kernel, parts(4), [], (place,), (own, x2, cx, x3, *arrived[2:], early_keep, early_other))
        turned = [jax.ShapeDtypeStruct((PLANE * rows, depth), jnp.bfloat16)] * 2
        high, low = call(turn_kernel, turned, [], (), (after(own, k2), x2, cx, x3))
        half = after(half, high)
        pack = call(add_kernel, [f32(rows, 3 * rows)], [], (), (half, far), flops=10**11)[0]
        return pack, high, low, *core_sum(k2, other, send)

    pack, high, low, t2, out2 = fenced(second_part, place, tuple(crossed), *mine, early_keep, early_other, o0, o1, e2, o2)
    ez, oz = both(pack, pack)
    y2 = xor(out2, 2)

    e3, o3, _, _ = lax.optimization_barrier((e3, o3, pack, y1))
    k3, other, send = call(third_kernel, parts(2), [], (), (high, low, e3, o3))
    c3 = xor(send, 1)
    y2 = call(copy_kernel, [f32(rows, 4 * rows)], [], (), (y2,), flops=5 * 10**9)[0]
    y3 = xor(after(other + c3[rows:], y2), 2)

    whole = f32(rows, (2 * reach + 1) * rows)
    band = call(functools.partial(band_kernel, reach), [whole], [], (place, pair_list), (t1, y1, t2, y2))[0]
    late = (k3, c3, y3, ez, oz)
    return pl.pallas_call(
        functools.partial(final_kernel, reach),
        in_specs=[pl.BlockSpec(memory_space=pltpu.SMEM)] * 2
        + [pl.BlockSpec(memory_space=pltpu.VMEM)] * len(late)
        + [pl.BlockSpec(memory_space=pl.ANY)],
        out_specs=pl.BlockSpec(memory_space=pl.ANY),
        out_shape=whole,
        scratch_shapes=[pltpu.VMEM((PLANE + 1, rows, rows), jnp.float32), pltpu.SemaphoreType.DMA((PLANE + 1,))],
        input_output_aliases={2 + len(late): 0},
        compiler_params=pltpu.CompilerParams(vmem_limit_bytes=VMEM_BYTES),
    )(place, pair_list, *late, band)


def solution(mesh):
    return jax.shard_map(
        functools.partial(body, mesh.shape["blk"]),
        mesh=mesh,
        in_specs=(P("blk", "groups"), P()),
        out_specs=P(("groups", "blk"), None),
        check_vma=False,
    )
```
